256 devices in a mesh: seq: 64 (over y_hi, x, z), head: 4 (over y_lo, core).
Axes of the slice: x: 4, y: 4 (y_hi: 2, y_lo: 2; y = y_hi * 2 + y_lo), z: 8, core: 2. Of those that a mesh axis runs over, the one named last changes fastest.
Arguments:
- queries: bfloat16 [32768, 4096], P('seq', 'head'), may hold values from -8 to 8
- keys: bfloat16 [32768, 4096], P('seq', 'head'), may hold values from -8 to 8
- values: bfloat16 [32768, 4096], P('seq', 'head'), may hold values from -6 to 6
- gates: int32 [64, 32, 6], P('seq', 'head'), may hold values from 0 to 63, as said below
- out_weight: bfloat16 [4096, 4096], P('head'), may hold values from -0.25 to 0.25
Outputs:
- mixed: bfloat16 [32768, 4096], P('seq', 'head')
The draws below stay inside these ranges and needn't reach their ends.
Inputs may be any that keep to these rules, and one draw needn't show every extreme that they name: gates[c, h, 0] = c; every other entry of (c, h) is c or a block before c; within one query block c and one group of heads g * 8 to g * 8 + 7, a block other than c is named at most once.
All inputs are finite; a program needn't handle non-finite values.
Results may differ from the reference program's by a relative error of at most 0.013.
Values may be sent and summed in bfloat16 or wider, within the bound.
No kernel may reach another device: no remote copies, remote signals or barrier semaphores. Data moves between devices by JAX's collectives and lax.ppermute only.
A program may use at most 192 MiB of HBM per device.

```python
import jax
import jax.numpy as jnp
from jax import lax

H = 32
HD = 128
D = 4096
BLOCK = 512
TOPK = 6
H_DEV = 8
NBLK = 64
TOKENS = 32768
N_HEAD = 4


def draw_queries(key, part):
    key = jax.random.fold_in(key, 101)
    result = jnp.clip(1.5 * jax.random.normal(key, (TOKENS, H, HD), jnp.float32), -8.0, 8.0)
    return result.reshape(TOKENS, H * HD).astype(jnp.bfloat16)


def draw_keys(key, part):
    key = jax.random.fold_in(key, 303)
    result = jnp.clip(1.5 * jax.random.normal(key, (TOKENS, H, HD), jnp.float32), -8.0, 8.0)
    return result.reshape(TOKENS, H * HD).astype(jnp.bfloat16)


def draw_gates(key, part):
    key = jax.random.fold_in(key, 202)
    block_range = jnp.arange(NBLK, dtype=jnp.int32)
    picks = H_DEV * (TOPK - 1)

    def single_cluster(group_key, segment_number):
        score_key, place_key = jax.random.split(group_key)
        noise = jax.random.randint(score_key, (NBLK,), 0, 1000)
        favour = jnp.where(block_range == 0, 1500, 0) + jnp.where(block_range >= segment_number - 3, 1000, 0)
        ranking = (noise + favour) * NBLK + block_range
        ranking = jnp.where(block_range < segment_number, ranking, -1 - block_range)
        order = jnp.argsort(-ranking).astype(jnp.int32)
        places = jnp.arange(picks, dtype=jnp.int32)
        listed = jnp.where(places < segment_number, order[jnp.minimum(places, NBLK - 1)], segment_number).astype(jnp.int32)
        spread = jax.random.permutation(place_key, picks)
        placed = listed[spread].reshape(H_DEV, TOPK - 1)
        own_column = jnp.full((H_DEV, 1), segment_number, jnp.int32)
        return jnp.concatenate([own_column, placed], axis=1)

    def one_block(segment_number):

        def one_head_group(group_index):
            group_key = jax.random.fold_in(jax.random.fold_in(key, segment_number), group_index)
            return single_cluster(group_key, segment_number)
        return jax.vmap(one_head_group)(jnp.arange(N_HEAD, dtype=jnp.int32)).reshape(H, TOPK)
    return jax.vmap(one_block)(block_range)


def levels(key, extent, cuts, smallest, high):
    gain, own = 1.0, jax.random.fold_in(key, 6)
    for axis_at, blocks in cuts:
        heights = jnp.exp(jax.random.uniform(jax.random.fold_in(own, axis_at), (blocks,), jnp.float32, smallest / len(cuts), high / len(cuts)))
        gain = gain * jnp.repeat(heights, extent[axis_at] // blocks).reshape([-1 if axis == axis_at else 1 for axis in range(len(extent))])
    return gain


def bell_draw(stream_key, shape, deviation, bound, shards=(), kind=jnp.bfloat16):
    array = jax.random.normal(stream_key, shape, jnp.float32) * deviation
    if len(shards) > 0:
        array = levels(stream_key, shape, shards, -0.22, 0.18) * array
    return jnp.clip(array, min=-bound, max=bound).astype(kind)


def setup_inputs(seed: int = 0) -> dict:
    streams_of = jax.random.split(jax.random.key(seed), 6)
    queries = draw_queries(jax.random.fold_in(streams_of[5], 71), 0)
    keys = draw_keys(jax.random.fold_in(streams_of[5], 71), 0)
    values = bell_draw(streams_of[2], (TOKENS, H * HD), 1.0, 6.0, ((0, 64), (1, 4)))
    gates = draw_gates(jax.random.fold_in(streams_of[5], 71), 0)
    out_weight = bell_draw(streams_of[4], (H * HD, D), (H * HD // 8) ** -0.5, 0.25, ((0, 4),))
    return dict(queries=queries, keys=keys, values=values, gates=gates, out_weight=out_weight)


NEGATIVE = -1.0e30


def reference(queries, keys, values, gates, out_weight):
    factor = HD ** -0.5
    key_blocks = keys.reshape(NBLK, BLOCK, H, HD).transpose(0, 2, 1, 3)
    value_blocks = values.reshape(NBLK, BLOCK, H, HD).transpose(0, 2, 1, 3)
    query_blocks = queries.reshape(NBLK, BLOCK, H, HD).transpose(0, 2, 1, 3)
    head_range = jnp.arange(H, dtype=jnp.int32)
    positions = jnp.arange(BLOCK, dtype=jnp.int32)
    causal = positions[None, :] <= positions[:, None]
    preceding_mask = jnp.tril(jnp.ones((TOPK, TOPK), dtype=bool), -1)

    def one_block(inputs):
        segment_number, chosen, query_part = inputs
        picked_keys = key_blocks[chosen, head_range[:, None]]
        picked_values = value_blocks[chosen, head_range[:, None]]
        scores = jnp.einsum("hqd,hjkd->hjqk", query_part.astype(jnp.float32), picked_keys.astype(jnp.float32)) * factor
        own_block = (chosen == segment_number)[:, :, None, None]
        allowed = jnp.logical_or(jnp.logical_not(own_block), causal[None, None])
        scores = jnp.where(allowed, scores, NEGATIVE)
        maxima = jnp.max(scores, axis=-1)
        score_exponent = jnp.exp(scores - maxima[..., None])
        totals = jnp.sum(score_exponent, axis=-1)
        rounded = lax.optimization_barrier(score_exponent.astype(jnp.bfloat16))
        partial_value = jnp.einsum("hjqk,hjkd->hjqd", rounded.astype(jnp.float32), picked_values.astype(jnp.float32)) / totals[..., None]
        partial_value = lax.optimization_barrier(partial_value.astype(jnp.bfloat16))
        repeat = jnp.any((chosen[:, :, None] == chosen[:, None, :]) & preceding_mask[None], axis=-1)
        counting = jnp.logical_not(repeat)[:, :, None]
        highest = jnp.max(jnp.where(counting, maxima, NEGATIVE), axis=1)
        weights = jnp.where(counting, totals * jnp.exp(jnp.where(counting, maxima - highest[:, None], 0.0)), 0.0)
        summed_output = jnp.einsum("hjq,hjqd->hqd", weights, partial_value.astype(jnp.float32))
        attended_values = (summed_output / jnp.sum(weights, axis=1)[..., None]).astype(jnp.bfloat16)
        return attended_values.transpose(1, 0, 2).reshape(BLOCK, H * HD)

    segment_count = lax.map(one_block, (jnp.arange(NBLK, dtype=jnp.int32), gates, query_blocks))
    attended_values = segment_count.reshape(TOKENS, H * HD)
    return jnp.dot(attended_values, out_weight, preferred_element_type=jnp.float32).astype(jnp.bfloat16)
```

```python
import functools
import math

import jax
import jax.numpy as jnp
from jax import lax
from jax.experimental import pallas as pl
from jax.experimental.pallas import tpu as pltpu
from jax.sharding import Mesh
from jax.sharding import PartitionSpec as P

NEGATIVE = -1e30
HEADS = 8
HD = 128
ROWS = 512
COLUMNS = 8
RING = 8
CHUNKS = 2
HC = HEADS // CHUNKS
STAT_ROWS = 32
PART_ROWS = HC * HD + STAT_ROWS
QB = 256
SCALE = HD**-0.5 * math.log2(math.e)
SEQ = ("yh", "x", "z")
HEAD = ("yl", "core")
PLANE = ("yh", "x")
NT = (((1,), (1,)), ((), ()))
TN = (((0,), (0,)), ((), ()))


def own_kernel(q_ref, k_ref, v_ref, o_ref, lse_ref):
    head = pl.program_id(0)
    k = k_ref[0]
    v = v_ref[0]
    for start in range(0, ROWS, QB):
        q = q_ref[0, start : start + QB, :]
        s = lax.dot_general(k, q, NT, preferred_element_type=jnp.float32)
        key_at = lax.broadcasted_iota(jnp.int32, s.shape, 0)
        query_at = lax.broadcasted_iota(jnp.int32, s.shape, 1) + start
        s = jnp.where(key_at <= query_at, s, NEGATIVE)
        top = jnp.max(s, axis=0, keepdims=True) * SCALE
        p = jnp.exp2(s * SCALE - top)
        total = jnp.sum(p, axis=0, keepdims=True)
        o = lax.dot_general(v, p.astype(jnp.bfloat16), TN, preferred_element_type=jnp.float32)
        o_ref[:, start : start + QB] = (o / total).astype(jnp.bfloat16)
        lse_ref[pl.ds(head, 1), start : start + QB] = top + jnp.log2(total)


def own_attention(q, k, v):
    block = pl.BlockSpec((1, ROWS, HD), lambda h: (h, 0, 0))
    return pl.pallas_call(
        own_kernel,
        grid=(HEADS,),
        in_specs=[block, block, block],
        out_specs=[
            pl.BlockSpec((HD, ROWS), lambda h: (h, 0)),
            pl.BlockSpec((HEADS, ROWS), lambda h: (0, 0)),
        ],
        out_shape=[
            jax.ShapeDtypeStruct((HEADS * HD, ROWS), jnp.bfloat16),
            jax.ShapeDtypeStruct((HEADS, ROWS), jnp.float32),
        ],
        cost_estimate=pl.CostEstimate(
            flops=HEADS * 4 * ROWS * ROWS * HD, bytes_accessed=4 << 20, transcendentals=HEADS * ROWS * ROWS
        ),
        name="own_block",
    )(q, k, v)


def task_kernel(table, q_ref, *refs):
    kv_refs = refs[: RING - 1]
    k_far, v_far, o_ref, acc, top, total, stat = refs[RING - 1 :]
    column = pl.program_id(0)
    acc[...] = jnp.zeros_like(acc)
    top[...] = jnp.full_like(top, NEGATIVE)
    total[...] = jnp.zeros_like(total)

    for place in range(RING):
        head = table[column, place]

        @pl.when((head >= 0) & (head < HC))
        def _(place=place, head=head):
            if place < RING - 1:
                k = kv_refs[place][0, head]
                v = kv_refs[place][1, head]
            else:
                k = k_far[head]
                v = v_far[head]
            row = pl.ds(head, 1)
            for start in range(0, ROWS, QB):
                span = slice(start, start + QB)
                q = q_ref[0, head, span, :]
                s = lax.dot_general(k, q, NT, preferred_element_type=jnp.float32)
                before = top[row, span]
                after = jnp.maximum(before, jnp.max(s, axis=0, keepdims=True) * SCALE)
                p = jnp.exp2(s * SCALE - after)
                keep = jnp.exp2(before - after)
                top[row, span] = after
                total[row, span] = total[row, span] * keep + jnp.sum(p, axis=0, keepdims=True)
                o = lax.dot_general(v, p.astype(jnp.bfloat16), TN, preferred_element_type=jnp.float32)
                acc[head, :, span] = acc[head, :, span] * keep + o

    sums = total[...]
    sums = jnp.where(sums > 0.0, sums, 1.0)
    for head in range(HC):
        o_ref[0, head * HD : (head + 1) * HD, :] = (acc[head] / sums[head : head + 1, :]).astype(jnp.bfloat16)
    lse = top[...] + jnp.log2(sums)
    first = lse.astype(jnp.bfloat16).astype(jnp.float32)
    second = (lse - first).astype(jnp.bfloat16).astype(jnp.float32)
    stat[...] = jnp.zeros_like(stat)
    stat[0:8, :] = first
    stat[8:16, :] = second
    stat[16:24, :] = lse - first - second
    o_ref[0, HC * HD : PART_ROWS, :] = stat[...].astype(jnp.bfloat16)


def column_tasks(table, q, kvs, k_far, v_far):
    whole = lambda *shape: pl.BlockSpec(shape, lambda c, t: (0,) * len(shape))
    return pl.pallas_call(
        task_kernel,
        grid_spec=pltpu.PrefetchScalarGridSpec(
            num_scalar_prefetch=1,
            grid=(COLUMNS,),
            in_specs=[pl.BlockSpec((1, HC, ROWS, HD), lambda c, t: (c, 0, 0, 0))]
            + [whole(2, HC, ROWS, HD)] * (RING - 1)
            + [whole(HC, ROWS, HD)] * 2,
            out_specs=pl.BlockSpec((1, PART_ROWS, ROWS), lambda c, t: (c, 0, 0)),
            scratch_shapes=[
                pltpu.VMEM((HC, HD, ROWS), jnp.float32),
                pltpu.VMEM((8, ROWS), jnp.float32),
                pltpu.VMEM((8, ROWS), jnp.float32),
                pltpu.VMEM((STAT_ROWS, ROWS), jnp.float32),
            ],
        ),
        out_shape=jax.ShapeDtypeStruct((COLUMNS, PART_ROWS, ROWS), jnp.bfloat16),
        compiler_params=pltpu.CompilerParams(vmem_limit_bytes=48 << 20),
        cost_estimate=pl.CostEstimate(
            flops=40 // CHUNKS * 4 * ROWS * ROWS * HD,
            bytes_accessed=16 << 20,
            transcendentals=40 // CHUNKS * ROWS * ROWS,
        ),
        name="column_tasks",
    )(table, q, *kvs, k_far, v_far)


def merge_kernel(first_head, part_ref, stat_ref, own_ref, own_lse_ref, o_ref):
    head = pl.program_id(0)
    stats = [stat_ref[i].astype(jnp.float32) for i in range(COLUMNS)]
    lse = [s[0:8] + s[8:16] + s[16:24] for s in stats]
    pick = lax.broadcasted_iota(jnp.int32, (8, ROWS), 0) == head
    lse = [jnp.max(jnp.where(pick, l, NEGATIVE), axis=0, keepdims=True) for l in lse]
    own = own_lse_ref[pl.ds(first_head + head, 1), :]
    highest = own
    for l in lse:
        highest = jnp.maximum(highest, l)
    weight = jnp.exp2(own - highest)
    norm = weight
    out = weight * own_ref[...].astype(jnp.float32)
    for i in range(COLUMNS):
        weight = jnp.exp2(lse[i] - highest)
        norm = norm + weight
        out = out + weight * part_ref[i].astype(jnp.float32)
    o_ref[...] = (out / norm).astype(jnp.bfloat16)


def merge(chunk, parts, own, own_lse):
    first = chunk * HC
    return pl.pallas_call(
        functools.partial(merge_kernel, first),
        grid=(HC,),
        in_specs=[
            pl.BlockSpec((COLUMNS, HD, ROWS), lambda h: (0, h, 0)),
            pl.BlockSpec((COLUMNS, STAT_ROWS, ROWS), lambda h: (0, HC * HD // STAT_ROWS, 0)),
            pl.BlockSpec((HD, ROWS), lambda h: (first + h, 0)),
            pl.BlockSpec((HEADS, ROWS), lambda h: (0, 0)),
        ],
        out_specs=pl.BlockSpec((HD, ROWS), lambda h: (h, 0)),
        out_shape=jax.ShapeDtypeStruct((HC * HD, ROWS), jnp.bfloat16),
        compiler_params=pltpu.CompilerParams(vmem_limit_bytes=32 << 20),
        cost_estimate=pl.CostEstimate(
            flops=COLUMNS * HC * HD * ROWS * 2, bytes_accessed=5 << 20, transcendentals=COLUMNS * HC * ROWS
        ),
        name="merge",
    )(parts, parts, own, own_lse)


def shift(array, axis, size, by):
    return lax.ppermute(array, axis, [(i, (i + by) % size) for i in range(size)])


def head_major(array):
    return array.reshape(ROWS, HEADS, HD).transpose(1, 0, 2)


def on_device(queries, keys, values, gates, out_weight):
    column = lax.axis_index("yh") * 4 + lax.axis_index("x")
    z = lax.axis_index("z")
    chip = lax.axis_index("yl")
    core = lax.axis_index("core")

    kv = jnp.stack([head_major(keys), head_major(values)])
    q = head_major(queries)
    chunk_of = lambda array, i, axis: lax.slice_in_dim(array, i * HC, (i + 1) * HC, axis=axis)

    plane_gates = lax.all_gather(gates, PLANE, axis=0, tiled=True)
    offsets = jnp.array([0, -1, 1, -2, 2, -3, 3, 4], jnp.int32)
    blocks = column * RING + (z + offsets + RING) % RING
    holders = jnp.arange(COLUMNS, dtype=jnp.int32) * RING + z
    named = jnp.any(plane_gates[:, :, None, 1:] == blocks[None, None, :, None], axis=-1)
    named = named & (blocks[None, None, :] != holders[:, None, None])
    head_range = jnp.arange(HEADS, dtype=jnp.int32)
    table = jnp.sum(jnp.where(named, head_range[None, :, None] + 1, 0), axis=1) - 1

    plane_q = [
        lax.all_gather(chunk_of(q, i, 0)[None], PLANE, axis=0, tiled=True) for i in range(CHUNKS)
    ]

    own, own_lse = own_attention(q, kv[0], kv[1])

    attended = []
    previous = None
    for i in range(CHUNKS):
        part = chunk_of(kv, i, 1)
        if previous is not None:
            part, _ = lax.optimization_barrier((part, previous))
        ups, downs = [part], [part]
        for _ in range(3):
            ups.append(shift(ups[-1], "z", RING, 1))
            downs.append(shift(downs[-1], "z", RING, -1))
        k_far = shift(ups[3][0], "z", RING, 1)
        v_far = shift(downs[3][1], "z", RING, -1)
        previous = (ups[3][0, 0, 0, 0], downs[3][0, 0, 0, 0])
        kvs = [part, ups[1], downs[1], ups[2], downs[2], ups[3], downs[3]]
        partial = column_tasks(table - i * HC, plane_q[i], kvs, k_far, v_far)
        back = lax.all_to_all(partial, PLANE, split_axis=0, concat_axis=0, tiled=True)
        attended.append(merge(i, back, own, own_lse))
    attended = jnp.concatenate(attended, axis=0)

    weight = out_weight.reshape(HEADS * HD, 2, 2048)

    def project(side):
        w = lax.dynamic_index_in_dim(weight, side, axis=1, keepdims=False)
        both = lax.dot_general(attended, w, TN, preferred_element_type=jnp.float32)
        both = both.reshape(ROWS, 2, 1024)
        mine = lax.dynamic_index_in_dim(both, core, axis=1, keepdims=False)
        other = lax.dynamic_index_in_dim(both, 1 - core, axis=1, keepdims=False)
        return mine + shift(other.astype(jnp.bfloat16), "core", 2, 1).astype(jnp.float32)

    away = shift(project(1 - chip).astype(jnp.bfloat16), "yl", 2, 1)
    return (project(chip) + away.astype(jnp.float32)).astype(jnp.bfloat16)


def solution(mesh):
    fine = Mesh(mesh.devices.reshape(2, 4, 8, 2, 2), SEQ + HEAD)
    placed = (
        P(SEQ, HEAD),
        P(SEQ, HEAD),
        P(SEQ, HEAD),
        P(SEQ, HEAD, None),
        P(HEAD, None),
    )
    return jax.shard_map(
        on_device, mesh=fine, in_specs=placed, out_specs=P(SEQ, HEAD), check_vma=False
    )
```

```python
import functools
import math

import jax
import jax.numpy as jnp
from jax import lax
from jax.experimental import pallas as pl
from jax.experimental.pallas import tpu as pltpu
from jax.sharding import Mesh
from jax.sharding import PartitionSpec as P

NEGATIVE = -1e30
HEADS = 8
HD = 128
ROWS = 512
COLUMNS = 8
RING = 8
STAT_ROWS = 32
HC = 2
CHUNKS = HEADS // HC
QB = 256
SCALE = HD**-0.5 * math.log2(math.e)
SEQ = ("yh", "x", "z")
HEAD = ("yl", "core")
PLANE = ("yh", "x")
NT = (((1,), (1,)), ((), ()))
TN = (((0,), (0,)), ((), ()))


def own_kernel(q_ref, k_ref, v_ref, o_ref, lse_ref):
    head = pl.program_id(0)
    k = k_ref[...]
    v = v_ref[...]
    for start in range(0, ROWS, QB):
        q = q_ref[start : start + QB, :]
        s = lax.dot_general(k, q, NT, preferred_element_type=jnp.float32)
        key_at = lax.broadcasted_iota(jnp.int32, s.shape, 0)
        query_at = lax.broadcasted_iota(jnp.int32, s.shape, 1) + start
        s = jnp.where(key_at <= query_at, s, NEGATIVE)
        top = jnp.max(s, axis=0, keepdims=True) * SCALE
        p = jnp.exp2(s * SCALE - top)
        total = jnp.sum(p, axis=0, keepdims=True)
        o = lax.dot_general(v, p.astype(jnp.bfloat16), TN, preferred_element_type=jnp.float32)
        o_ref[:, start : start + QB] = (o / total).astype(jnp.bfloat16)
        lse_ref[pl.ds(head, 1), start : start + QB] = top + jnp.log2(total)


def own_attention(q, k, v):
    block = pl.BlockSpec((ROWS, HD), lambda h: (0, h))
    return pl.pallas_call(
        own_kernel,
        grid=(HEADS,),
        in_specs=[block, block, block],
        out_specs=[
            pl.BlockSpec((HD, ROWS), lambda h: (h, 0)),
            pl.BlockSpec((HEADS, ROWS), lambda h: (0, 0)),
        ],
        out_shape=[
            jax.ShapeDtypeStruct((HEADS * HD, ROWS), jnp.bfloat16),
            jax.ShapeDtypeStruct((HEADS, ROWS), jnp.float32),
        ],
        cost_estimate=pl.CostEstimate(
            flops=9 * 10**9, bytes_accessed=4 << 20, transcendentals=0
        ),
        name="own_block",
    )(q, k, v)


def task_kernel(q_row, kv_count, has_next, table, q_hbm, own_ref, *refs):
    heads = HC
    next_ref = refs[0] if has_next else None
    kv_hbm = refs[has_next : has_next + kv_count]
    o_ref, q_buf, kv_buf, acc, top, total, stat, scores, tops, tasks, sems = refs[-11:]
    own_column = table[COLUMNS, 0]
    moves = [(q_hbm.at[:, q_row : q_row + heads * HD], q_buf)]
    if kv_count == 1:
        moves += [(kv_hbm[0], kv_buf)]
    else:
        moves += [(kv_hbm[i], kv_buf.at[i]) for i in range(RING - 1)]
        moves += [(kv_hbm[RING - 1 + i], kv_buf.at[RING - 1, i]) for i in range(2)]
    copies = [pltpu.make_async_copy(*move, sems.at[i]) for i, move in enumerate(moves)]
    for copy in copies:
        copy.start()

    def clear(i, _):
        acc[i] = jnp.zeros((HD, ROWS), jnp.float32)
        return 0

    lax.fori_loop(0, COLUMNS * heads, clear, 0)
    top[...] = jnp.full_like(top, NEGATIVE)
    total[...] = jnp.zeros_like(total)

    def collect(i, count):
        head = table[i // RING, i % RING]
        wanted = (head >= 0) & (head < heads)

        @pl.when(wanted)
        def _():
            tasks[0, count] = i // RING
            tasks[1, count] = i % RING
            tasks[2, count] = head
            tasks[3, count] = (i // RING) * heads + head

        return count + wanted.astype(jnp.int32)

    count = lax.fori_loop(0, COLUMNS * RING, collect, 0)
    for extra in range(3):
        tasks[0, count + extra] = 0
        tasks[1, count + extra] = 0
        tasks[2, count + extra] = 0
        tasks[3, count + extra] = COLUMNS * heads
    for copy in copies:
        copy.wait()
    q_buf[own_column] = own_ref[...]

    def lanes(t):
        return pl.ds(pl.multiple_of(tasks[2, t] * HD, HD), HD)

    def score(t, slot):
        k = kv_buf[tasks[1, t], 0, :, lanes(t)]
        q = q_buf[tasks[0, t], lanes(t), :]
        s = jnp.dot(k, q, preferred_element_type=jnp.float32)
        scores[slot] = s
        tops[slot] = jnp.max(s, axis=0, keepdims=True) * SCALE

    def soften(t, slot):
        place = tasks[3, t]
        before = top[place]
        after = jnp.maximum(before, tops[slot])
        p = jnp.exp2(scores[slot] * SCALE - after)
        keep = jnp.exp2(before - after)
        top[place] = after
        total[place] = total[place] * keep + jnp.sum(p, axis=0, keepdims=True)
        v = kv_buf[tasks[1, t], 1, :, lanes(t)]
        o = lax.dot_general(v, p.astype(jnp.bfloat16), TN, preferred_element_type=jnp.float32)
        acc[place] = acc[place] * keep + o

    score(0, 0)

    def two(u, _):
        t = u * 2
        score(t + 1, 1)
        soften(t, 0)
        score(t + 2, 0)
        soften(t + 1, 1)
        return 0

    lax.fori_loop(0, (count + 1) // 2, two, 0)

    stat[...] = jnp.zeros_like(stat)

    def finish(column, _):
        for head in range(heads):
            place = column * heads + head
            sums = total[place]
            sums = jnp.where(sums > 0.0, sums, 1.0)
            o_ref[column, head * HD : (head + 1) * HD, :] = (acc[place] / sums).astype(jnp.bfloat16)
            lse = top[place] + jnp.log2(sums)
            first = lse.astype(jnp.bfloat16).astype(jnp.float32)
            second = (lse - first).astype(jnp.bfloat16).astype(jnp.float32)
            stat[head : head + 1, :] = first
            stat[8 + head : 9 + head, :] = second
            stat[16 + head : 17 + head, :] = lse - first - second
        o_ref[column, heads * HD : heads * HD + STAT_ROWS, :] = stat[...].astype(jnp.bfloat16)
        return 0

    lax.fori_loop(own_column, COLUMNS, finish, 0)

    def forward(column, _):
        if has_next:
            o_ref[column, 0 : heads * HD, :] = next_ref[...]
        else:
            o_ref[column, 0 : heads * HD, :] = jnp.zeros((heads * HD, ROWS), jnp.bfloat16)
        o_ref[column, heads * HD : heads * HD + STAT_ROWS, :] = jnp.zeros((STAT_ROWS, ROWS), jnp.bfloat16)
        return 0

    lax.fori_loop(0, own_column, forward, 0)


def column_tasks(chunk, table, q, q_row, q_turned, following, kvs, after):
    heads = HC
    anywhere = pl.BlockSpec(memory_space=pltpu.HBM)
    turned = lambda at: pl.BlockSpec((heads * HD, ROWS), lambda i, t: (at, 0))
    rows = heads * HD + STAT_ROWS
    has_next = following is not None
    return pl.pallas_call(
        functools.partial(task_kernel, q_row, len(kvs), int(has_next)),
        grid_spec=pltpu.PrefetchScalarGridSpec(
            num_scalar_prefetch=1,
            grid=(1,),
            in_specs=[anywhere, turned(chunk)]
            + ([turned(following)] if has_next else [])
            + [anywhere] * (len(kvs) + len(after)),
            out_specs=pl.BlockSpec((COLUMNS, rows, ROWS), lambda i, t: (0, 0, 0)),
            scratch_shapes=[
                pltpu.VMEM((COLUMNS, heads * HD, ROWS), jnp.bfloat16),
                pltpu.VMEM((RING, 2, ROWS, heads * HD), jnp.bfloat16),
                pltpu.VMEM((COLUMNS * heads + 1, HD, ROWS), jnp.float32),
                pltpu.VMEM((COLUMNS * heads + 1, 1, ROWS), jnp.float32),
                pltpu.VMEM((COLUMNS * heads + 1, 1, ROWS), jnp.float32),
                pltpu.VMEM((STAT_ROWS, ROWS), jnp.float32),
                pltpu.VMEM((2, ROWS, ROWS), jnp.float32),
                pltpu.VMEM((2, 1, ROWS), jnp.float32),
                pltpu.SMEM((4, COLUMNS * RING + 8), jnp.int32),
                pltpu.SemaphoreType.DMA((RING + 2,)),
            ],
        ),
        out_shape=jax.ShapeDtypeStruct((COLUMNS, rows, ROWS), jnp.bfloat16),
        compiler_params=pltpu.CompilerParams(vmem_limit_bytes=56 << 20),
        cost_estimate=pl.CostEstimate(
            flops=heads * 4 * 10**9,
            bytes_accessed=heads * 4 << 20,
            transcendentals=0,
        ),
        name="column_tasks",
    )(table, q, q_turned, *([q_turned] if has_next else []), *kvs, *after)


def merge_kernel(first_head, column, part_ref, stat_ref, own_ref, own_lse_ref, o_ref):
    head = pl.program_id(0)
    stats = [stat_ref[i].astype(jnp.float32) for i in range(COLUMNS)]
    lse = [jnp.where(i <= column[0], s[0:8] + s[8:16] + s[16:24], NEGATIVE) for i, s in enumerate(stats)]
    pick = lax.broadcasted_iota(jnp.int32, (8, ROWS), 0) == head
    lse = [jnp.max(jnp.where(pick, l, NEGATIVE), axis=0, keepdims=True) for l in lse]
    own = own_lse_ref[pl.ds(first_head + head, 1), :]
    highest = own
    for l in lse:
        highest = jnp.maximum(highest, l)
    weight = jnp.exp2(own - highest)
    norm = weight
    out = weight * own_ref[...].astype(jnp.float32)
    for i in range(COLUMNS):
        weight = jnp.exp2(lse[i] - highest)
        norm = norm + weight
        out = out + weight * part_ref[i].astype(jnp.float32)
    o_ref[...] = (out / norm).astype(jnp.bfloat16)


def merge(chunk, column, parts, own, own_lse):
    return pl.pallas_call(
        functools.partial(merge_kernel, chunk * HC),
        grid_spec=pltpu.PrefetchScalarGridSpec(
            num_scalar_prefetch=1,
            grid=(HC,),
            in_specs=[
                pl.BlockSpec((COLUMNS, HD, ROWS), lambda h, c: (0, h, 0)),
                pl.BlockSpec((COLUMNS, STAT_ROWS, ROWS), lambda h, c: (0, HC * HD // STAT_ROWS, 0)),
                pl.BlockSpec((HD, ROWS), lambda h, c: (chunk * HC + h, 0)),
                pl.BlockSpec((HEADS, ROWS), lambda h, c: (0, 0)),
            ],
            out_specs=pl.BlockSpec((HD, ROWS), lambda h, c: (h, 0)),
        ),
        out_shape=jax.ShapeDtypeStruct((HC * HD, ROWS), jnp.bfloat16),
        compiler_params=pltpu.CompilerParams(vmem_limit_bytes=20 << 20),
        cost_estimate=pl.CostEstimate(flops=0, bytes_accessed=HC * 5 << 20, transcendentals=0),
        name="merge",
    )(column, parts, parts, own, own_lse)


def pack_kernel(*refs):
    o_ref = refs[-1]
    for i in range(o_ref.shape[0]):
        o_ref[i] = refs[i][...]


def pack(first, heads, arrays, after):
    block = pl.BlockSpec((ROWS, heads * HD), lambda i: (0, first // heads))
    shape = (len(arrays), ROWS, heads * HD)
    return pl.pallas_call(
        pack_kernel,
        grid=(1,),
        in_specs=[block] * len(arrays) + [pl.BlockSpec(memory_space=pltpu.HBM)] * len(after),
        out_specs=pl.BlockSpec(shape, lambda i: (0, 0, 0)),
        out_shape=jax.ShapeDtypeStruct(shape, jnp.bfloat16),
        cost_estimate=pl.CostEstimate(flops=0, bytes_accessed=heads << 20, transcendentals=0),
        name="pack",
    )(*arrays, *after)


def halves_kernel(up_ref, down_ref, *refs):
    k_ref, v_ref = refs[-2:]
    k_ref[...] = up_ref[0]
    v_ref[...] = down_ref[0]


def hold_kernel(up_ref, down_ref, *refs):
    for source, target in ((up_ref, refs[-2]), (down_ref, refs[-1])):
        target[...] = source[...]


def hold(up, down, after):
    whole = pl.BlockSpec(up.shape, lambda i: (0, 0, 0))
    return pl.pallas_call(
        hold_kernel,
        grid=(1,),
        in_specs=[whole, whole] + [pl.BlockSpec(memory_space=pltpu.HBM)] * len(after),
        out_specs=[whole, whole],
        out_shape=[jax.ShapeDtypeStruct(up.shape, up.dtype)] * 2,
        cost_estimate=pl.CostEstimate(flops=0, bytes_accessed=4 << 20, transcendentals=0),
        name="hold",
    )(up, down, *after)


def far_halves(up, down, after):
    shape = up.shape[1:]
    whole = pl.BlockSpec(shape, lambda i: (0, 0))
    return pl.pallas_call(
        halves_kernel,
        grid=(1,),
        in_specs=[
            pl.BlockSpec((1,) + shape, lambda i: (0, 0, 0)),
            pl.BlockSpec((1,) + shape, lambda i: (1, 0, 0)),
        ]
        + [pl.BlockSpec(memory_space=pltpu.HBM)] * len(after),
        out_specs=[whole, whole],
        out_shape=[jax.ShapeDtypeStruct(shape, up.dtype)] * 2,
        cost_estimate=pl.CostEstimate(flops=0, bytes_accessed=2 << 20, transcendentals=0),
        name="far_halves",
    )(up, down, *after)


def shift(array, axis, size, by):
    return lax.ppermute(array, axis, [(i, (i + by) % size) for i in range(size)])


def on_device(queries, keys, values, gates, out_weight):
    column = lax.axis_index("yh") * 4 + lax.axis_index("x")
    z = lax.axis_index("z")
    chip = lax.axis_index("yl")
    core = lax.axis_index("core")

    gate_rows = jnp.zeros((STAT_ROWS, ROWS), jnp.bfloat16)
    gate_rows = lax.dynamic_update_slice(gate_rows, gates[0].astype(jnp.bfloat16), (0, 0))
    q_turned = queries.T
    at_first = jnp.concatenate([q_turned[: 2 * HC * HD], gate_rows], axis=0)

    def exchange(parts):
        return lax.all_to_all(parts, PLANE, split_axis=0, concat_axis=0, tiled=True)

    plane_q = exchange(jnp.broadcast_to(at_first[None], (COLUMNS,) + at_first.shape))
    plane_gates = plane_q[:, 2 * HC * HD : 2 * HC * HD + HEADS, 0:6].astype(jnp.int32)
    columns = jnp.arange(COLUMNS, dtype=jnp.int32)
    plane_gates = jnp.where((columns > column)[:, None, None], plane_gates, -1)
    plane_gates = jnp.where((columns == column)[:, None, None], gates, plane_gates)
    holders = jnp.arange(COLUMNS, dtype=jnp.int32) * RING + z
    head_range = jnp.arange(HEADS, dtype=jnp.int32)

    def table_of(places):
        blocks = column * RING + places
        named = jnp.any(plane_gates[:, :, None, 1:] == blocks[None, None, :, None], axis=-1)
        named = named & (blocks[None, None, :] != holders[:, None, None])
        table = jnp.sum(jnp.where(named, head_range[None, :, None] + 1, 0), axis=1) - 1
        return jnp.concatenate([table, jnp.full((1, RING), column, jnp.int32)], axis=0)

    ring_table = table_of((z + jnp.array([0, -1, 1, -2, 2, -3, 3, 4], jnp.int32) + RING) % RING)
    line_table = table_of(jnp.arange(RING, dtype=jnp.int32))

    own, own_lse = own_attention(queries, keys, values)

    def weight_part(side, half):
        return lax.dynamic_slice_in_dim(out_weight, side * 2048 + half * 1024, 1024, axis=1)

    weights = [weight_part(s, c) for s in (1 - chip, chip) for c in (1 - core, core)]

    def gather_kv(part):
        return [lax.all_gather(part[None], "z", axis=0, tiled=True)]

    def start_kv(chunk, after):
        part = pack(chunk * HC, HC, [keys, values], after)
        return [part]

    def move_kv(ring, after=None):
        up, down = ring[-2:] if len(ring) > 1 else ring * 2
        if after is not None:
            up, down = hold(up, down, after)
        return ring + [shift(up, "z", RING, 1), shift(down, "z", RING, -1)]

    def complete_kv(ring, after):
        k_half, v_half = far_halves(ring[5], ring[6], after)
        return ring + [shift(k_half, "z", RING, 1), shift(v_half, "z", RING, -1)]

    first_column = column.reshape(1)

    def serve(chunk, table, q, q_row, following, kvs, after):
        return column_tasks(
            chunk, table - jnp.int32(chunk * HC) * below, q, q_row, q_turned, following, kvs, after
        )

    below = (jnp.arange(COLUMNS + 1) < COLUMNS).astype(jnp.int32)[:, None]
    def swap_core(array):
        return shift(array, "core", 2, 1)

    def swap_chip(array):
        return shift(array, "yl", 2, 1)

    def weight_part(first, last, side, half):
        return lax.dynamic_slice(out_weight, (first, (side * 2 + half) * 1024), (last - first, 1024))

    rows = HC * HD

    sides = (1 - chip, chip)
    weights = [(weight_part(0, HEADS * HD, side, core), swap_core(weight_part(0, HEADS * HD, side, 1 - core))) for side in sides]

    def project(chunk, count, features):
        both = jnp.concatenate([features, swap_core(features)], axis=0)
        place = slice(chunk * rows, (chunk + count) * rows)
        return [
            lax.dot_general(both, jnp.concatenate([w[place] for w in pair], axis=0), TN, preferred_element_type=jnp.float32)
            for pair in weights
        ]

    def merged(chunk, back):
        return merge(chunk, first_column, back, own, own_lse)

    kv0 = gather_kv(start_kv(0, [])[0])
    ring1 = move_kv(move_kv(start_kv(1, [own])))
    part0 = serve(0, line_table, plane_q, 0, 2, kv0, ring1[-2:])
    back0 = exchange(part0)
    ring1 = move_kv(ring1)
    kv2 = gather_kv(start_kv(2, [kv0[0], *ring1[-2:]])[0])
    kv1 = complete_kv(ring1, [])
    part1 = serve(1, ring_table, plane_q, HC * HD, 3, kv1, [part0])
    back1 = exchange(part1)
    ring3 = move_kv(move_kv(start_kv(3, [part1])))
    part2 = serve(2, line_table, back0, 0, None, kv2, [part1])
    back2 = exchange(part2)
    kv3 = complete_kv(move_kv(ring3), [part2])
    sums = project(0, 2, jnp.concatenate([merged(0, back0), merged(1, back1)], axis=0))
    part3 = serve(3, ring_table, back1, 0, None, kv3, [part2, *sums])
    back3 = exchange(part3)
    for chunk, back in ((2, back2), (3, back3)):
        sums = [a + b for a, b in zip(sums, project(chunk, 1, merged(chunk, back)))]
    away = swap_chip(sums[0].astype(jnp.bfloat16))
    return (sums[1] + away.astype(jnp.float32)).astype(jnp.bfloat16)


def solution(mesh):
    fine = Mesh(mesh.devices.reshape(2, 4, 8, 2, 2), SEQ + HEAD)
    placed = (
        P(SEQ, HEAD),
        P(SEQ, HEAD),
        P(SEQ, HEAD),
        P(SEQ, HEAD, None),
        P(HEAD, None),
    )
    return jax.shard_map(
        on_device, mesh=fine, in_specs=placed, out_specs=P(SEQ, HEAD), check_vma=False
    )
```

```python
import functools
import math

import jax
import jax.numpy as jnp
from jax import lax
from jax.experimental import pallas as pl
from jax.experimental.pallas import tpu as pltpu
from jax.sharding import Mesh
from jax.sharding import PartitionSpec as P

NEGATIVE = -1e30
HEADS = 8
HD = 128
ROWS = 512
COLUMNS = 8
RING = 8
STAT_ROWS = 16
HC = 2
CHUNKS = HEADS // HC
QB = 256
SCALE = HD**-0.5 * math.log2(math.e)
SEQ = ("yh", "x", "z")
HEAD = ("yl", "core")
PLANE = ("yh", "x")
NT = (((1,), (1,)), ((), ()))
TN = (((0,), (0,)), ((), ()))


def own_kernel(q_ref, k_ref, v_ref, _, o_ref, lse_ref):
    head = pl.program_id(0)
    k = k_ref[...]
    v = v_ref[...]
    for start in range(0, ROWS, QB):
        q = q_ref[start : start + QB, :]
        s = lax.dot_general(k, q, NT, preferred_element_type=jnp.float32)
        key_at = lax.broadcasted_iota(jnp.int32, s.shape, 0)
        query_at = lax.broadcasted_iota(jnp.int32, s.shape, 1) + start
        s = jnp.where(key_at <= query_at, s, NEGATIVE)
        top = jnp.max(s, axis=0, keepdims=True) * SCALE
        p = jnp.exp2(s * SCALE - top)
        total = jnp.sum(p, axis=0, keepdims=True)
        o = lax.dot_general(v, p.astype(jnp.bfloat16), TN, preferred_element_type=jnp.float32)
        o_ref[:, start : start + QB] = (o / total).astype(jnp.bfloat16)
        lse_ref[pl.ds(head, 1), start : start + QB] = top + jnp.log2(total)


def own_attention(q, k, v, after):
    block = pl.BlockSpec((ROWS, HD), lambda h: (0, h))
    return pl.pallas_call(
        own_kernel,
        grid=(HEADS,),
        in_specs=[block, block, block, pl.BlockSpec(memory_space=pltpu.HBM)],
        out_specs=[
            pl.BlockSpec((HD, ROWS), lambda h: (h, 0)),
            pl.BlockSpec((HEADS, ROWS), lambda h: (0, 0)),
        ],
        out_shape=[
            jax.ShapeDtypeStruct((HEADS * HD, ROWS), jnp.bfloat16),
            jax.ShapeDtypeStruct((HEADS, ROWS), jnp.float32),
        ],
        cost_estimate=pl.CostEstimate(
            flops=9 * 10**9, bytes_accessed=4 << 20, transcendentals=0
        ),
        name="own_block",
    )(q, k, v, after)


def task_kernel(q_row, kv_count, has_next, table, q_hbm, own_ref, *refs):
    heads = HC
    next_ref = refs[0] if has_next else None
    kv_hbm = refs[has_next : has_next + kv_count]
    o_ref, q_buf, kv_buf, acc, top, total, stat, scores, tops, tasks, sems = refs[-11:]
    own_column = table[COLUMNS, 0]
    moves = [(q_hbm.at[:, q_row : q_row + heads * HD], q_buf)]
    if kv_count == 1:
        moves += [(kv_hbm[0], kv_buf)]
    else:
        moves += [(kv_hbm[i], kv_buf.at[i]) for i in range(RING - 1)]
        moves += [(kv_hbm[RING - 1 + i], kv_buf.at[RING - 1, i]) for i in range(2)]
    copies = [pltpu.make_async_copy(*move, sems.at[i]) for i, move in enumerate(moves)]
    for copy in copies:
        copy.start()

    def clear(i, _):
        acc[i] = jnp.zeros((HD, ROWS), jnp.float32)
        return 0

    lax.fori_loop(0, COLUMNS * heads, clear, 0)
    top[...] = jnp.full_like(top, NEGATIVE)
    total[...] = jnp.zeros_like(total)

    def collect(i, count):
        head = table[i // RING, i % RING]
        wanted = (head >= 0) & (head < heads)

        @pl.when(wanted)
        def _():
            tasks[0, count] = i // RING
            tasks[1, count] = i % RING
            tasks[2, count] = head
            tasks[3, count] = (i // RING) * heads + head

        return count + wanted.astype(jnp.int32)

    count = lax.fori_loop(0, COLUMNS * RING, collect, 0)
    for extra in range(3):
        tasks[0, count + extra] = 0
        tasks[1, count + extra] = 0
        tasks[2, count + extra] = 0
        tasks[3, count + extra] = COLUMNS * heads
    for copy in copies:
        copy.wait()
    q_buf[own_column] = own_ref[...]

    def lanes(t):
        return pl.ds(pl.multiple_of(tasks[2, t] * HD, HD), HD)

    def score(t, slot):
        k = kv_buf[tasks[1, t], 0, :, lanes(t)]
        q = q_buf[tasks[0, t], lanes(t), :]
        s = jnp.dot(k, q, preferred_element_type=jnp.float32)
        scores[slot] = s
        tops[slot] = jnp.max(s, axis=0, keepdims=True) * SCALE

    def soften(t, slot):
        place = tasks[3, t]
        before = top[place]
        after = jnp.maximum(before, tops[slot])
        p = jnp.exp2(scores[slot] * SCALE - after)
        keep = jnp.exp2(before - after)
        top[place] = after
        total[place] = total[place] * keep + jnp.sum(p, axis=0, keepdims=True)
        v = kv_buf[tasks[1, t], 1, :, lanes(t)]
        o = lax.dot_general(v, p.astype(jnp.bfloat16), TN, preferred_element_type=jnp.float32)
        acc[place] = acc[place] * keep + o

    score(0, 0)

    def two(u, _):
        t = u * 2
        score(t + 1, 1)
        soften(t, 0)
        score(t + 2, 0)
        soften(t + 1, 1)
        return 0

    lax.fori_loop(0, (count + 1) // 2, two, 0)

    stat[...] = jnp.zeros_like(stat)

    def finish(column, _):
        for head in range(heads):
            place = column * heads + head
            sums = total[place]
            sums = jnp.where(sums > 0.0, sums, 1.0)
            o_ref[column, head * HD : (head + 1) * HD, :] = (acc[place] / sums).astype(jnp.bfloat16)
            lse = top[place] + jnp.log2(sums)
            first = lse.astype(jnp.bfloat16).astype(jnp.float32)
            second = (lse - first).astype(jnp.bfloat16).astype(jnp.float32)
            for piece, value in enumerate((first, second, lse - first - second)):
                row = piece * heads + head
                stat[row : row + 1, :] = value
        o_ref[column, heads * HD : heads * HD + STAT_ROWS, :] = stat[...].astype(jnp.bfloat16)
        return 0

    lax.fori_loop(own_column, COLUMNS, finish, 0)

    def forward(column, _):
        if has_next:
            o_ref[column, 0 : heads * HD, :] = next_ref[...]
        else:
            o_ref[column, 0 : heads * HD, :] = jnp.zeros((heads * HD, ROWS), jnp.bfloat16)
        o_ref[column, heads * HD : heads * HD + STAT_ROWS, :] = jnp.zeros((STAT_ROWS, ROWS), jnp.bfloat16)
        return 0

    lax.fori_loop(0, own_column, forward, 0)


def column_tasks(chunk, table, q, q_row, q_turned, following, kvs, after):
    heads = HC
    anywhere = pl.BlockSpec(memory_space=pltpu.HBM)
    turned = lambda at: pl.BlockSpec((heads * HD, ROWS), lambda i, t: (at, 0))
    rows = heads * HD + STAT_ROWS
    has_next = following is not None
    return pl.pallas_call(
        functools.partial(task_kernel, q_row, len(kvs), int(has_next)),
        grid_spec=pltpu.PrefetchScalarGridSpec(
            num_scalar_prefetch=1,
            grid=(1,),
            in_specs=[anywhere, turned(chunk)]
            + ([turned(following)] if has_next else [])
            + [anywhere] * (len(kvs) + len(after)),
            out_specs=pl.BlockSpec((COLUMNS, rows, ROWS), lambda i, t: (0, 0, 0)),
            scratch_shapes=[
                pltpu.VMEM((COLUMNS, heads * HD, ROWS), jnp.bfloat16),
                pltpu.VMEM((RING, 2, ROWS, heads * HD), jnp.bfloat16),
                pltpu.VMEM((COLUMNS * heads + 1, HD, ROWS), jnp.float32),
                pltpu.VMEM((COLUMNS * heads + 1, 1, ROWS), jnp.float32),
                pltpu.VMEM((COLUMNS * heads + 1, 1, ROWS), jnp.float32),
                pltpu.VMEM((STAT_ROWS, ROWS), jnp.float32),
                pltpu.VMEM((2, ROWS, ROWS), jnp.float32),
                pltpu.VMEM((2, 1, ROWS), jnp.float32),
                pltpu.SMEM((4, COLUMNS * RING + 8), jnp.int32),
                pltpu.SemaphoreType.DMA((RING + 2,)),
            ],
        ),
        out_shape=jax.ShapeDtypeStruct((COLUMNS, rows, ROWS), jnp.bfloat16),
        compiler_params=pltpu.CompilerParams(vmem_limit_bytes=56 << 20),
        cost_estimate=pl.CostEstimate(
            flops=heads * 4 * 10**9,
            bytes_accessed=heads * 4 << 20,
            transcendentals=0,
        ),
        name="column_tasks",
    )(table, q, q_turned, *([q_turned] if has_next else []), *kvs, *after)


def merge_kernel(first_head, column, part_ref, stat_ref, own_ref, own_lse_ref, o_ref):
    head = pl.program_id(0)
    row = lax.broadcasted_iota(jnp.int32, (STAT_ROWS, ROWS), 0)
    pick = (row < 3 * HC) & (row % HC == head)
    lse = []
    for i in range(COLUMNS):
        pieces = jnp.where(pick, stat_ref[i].astype(jnp.float32), 0.0)
        lse.append(jnp.where(i <= column[0], jnp.sum(pieces, axis=0, keepdims=True), NEGATIVE))
    own = own_lse_ref[pl.ds(first_head + head, 1), :]
    highest = own
    for l in lse:
        highest = jnp.maximum(highest, l)
    weight = jnp.exp2(own - highest)
    norm = weight
    out = weight * own_ref[...].astype(jnp.float32)
    for i in range(COLUMNS):
        weight = jnp.exp2(lse[i] - highest)
        norm = norm + weight
        out = out + weight * part_ref[i].astype(jnp.float32)
    o_ref[...] = (out / norm).astype(jnp.bfloat16)


def merge(chunk, column, parts, own, own_lse):
    return pl.pallas_call(
        functools.partial(merge_kernel, chunk * HC),
        grid_spec=pltpu.PrefetchScalarGridSpec(
            num_scalar_prefetch=1,
            grid=(HC,),
            in_specs=[
                pl.BlockSpec((COLUMNS, HD, ROWS), lambda h, c: (0, h, 0)),
                pl.BlockSpec((COLUMNS, STAT_ROWS, ROWS), lambda h, c: (0, HC * HD // STAT_ROWS, 0)),
                pl.BlockSpec((HD, ROWS), lambda h, c: (chunk * HC + h, 0)),
                pl.BlockSpec((HEADS, ROWS), lambda h, c: (0, 0)),
            ],
            out_specs=pl.BlockSpec((HD, ROWS), lambda h, c: (h, 0)),
        ),
        out_shape=jax.ShapeDtypeStruct((HC * HD, ROWS), jnp.bfloat16),
        compiler_params=pltpu.CompilerParams(vmem_limit_bytes=20 << 20),
        cost_estimate=pl.CostEstimate(flops=0, bytes_accessed=HC * 5 << 20, transcendentals=0),
        name="merge",
    )(column, parts, parts, own, own_lse)


def pack_kernel(*refs):
    o_ref = refs[-1]
    for i in range(o_ref.shape[0]):
        o_ref[i] = refs[i][...]


def pack(first, heads, arrays, after):
    block = pl.BlockSpec((ROWS, heads * HD), lambda i: (0, first // heads))
    shape = (len(arrays), ROWS, heads * HD)
    return pl.pallas_call(
        pack_kernel,
        grid=(1,),
        in_specs=[block] * len(arrays) + [pl.BlockSpec(memory_space=pltpu.HBM)] * len(after),
        out_specs=pl.BlockSpec(shape, lambda i: (0, 0, 0)),
        out_shape=jax.ShapeDtypeStruct(shape, jnp.bfloat16),
        cost_estimate=pl.CostEstimate(flops=0, bytes_accessed=heads << 20, transcendentals=0),
        name="pack",
    )(*arrays, *after)


def halves_kernel(up_ref, down_ref, *refs):
    k_ref, v_ref = refs[-2:]
    k_ref[...] = up_ref[0]
    v_ref[...] = down_ref[0]


def hold_kernel(up_ref, down_ref, *refs):
    for source, target in ((up_ref, refs[-2]), (down_ref, refs[-1])):
        target[...] = source[...]


def hold(up, down, after):
    whole = pl.BlockSpec(up.shape, lambda i: (0, 0, 0))
    return pl.pallas_call(
        hold_kernel,
        grid=(1,),
        in_specs=[whole, whole] + [pl.BlockSpec(memory_space=pltpu.HBM)] * len(after),
        out_specs=[whole, whole],
        out_shape=[jax.ShapeDtypeStruct(up.shape, up.dtype)] * 2,
        cost_estimate=pl.CostEstimate(flops=0, bytes_accessed=4 << 20, transcendentals=0),
        name="hold",
    )(up, down, *after)


def far_halves(up, down, after):
    shape = up.shape[1:]
    whole = pl.BlockSpec(shape, lambda i: (0, 0))
    return pl.pallas_call(
        halves_kernel,
        grid=(1,),
        in_specs=[
            pl.BlockSpec((1,) + shape, lambda i: (0, 0, 0)),
            pl.BlockSpec((1,) + shape, lambda i: (1, 0, 0)),
        ]
        + [pl.BlockSpec(memory_space=pltpu.HBM)] * len(after),
        out_specs=[whole, whole],
        out_shape=[jax.ShapeDtypeStruct(shape, up.dtype)] * 2,
        cost_estimate=pl.CostEstimate(flops=0, bytes_accessed=2 << 20, transcendentals=0),
        name="far_halves",
    )(up, down, *after)


def shift(array, axis, size, by):
    return lax.ppermute(array, axis, [(i, (i + by) % size) for i in range(size)])


def on_device(queries, keys, values, gates, out_weight):
    column = lax.axis_index("yh") * 4 + lax.axis_index("x")
    z = lax.axis_index("z")
    chip = lax.axis_index("yl")
    core = lax.axis_index("core")

    gate_rows = jnp.zeros((STAT_ROWS, ROWS), jnp.bfloat16)
    gate_rows = lax.dynamic_update_slice(gate_rows, gates[0].astype(jnp.bfloat16), (0, 0))
    q_turned = queries.T
    at_first = jnp.concatenate([q_turned[: 2 * HC * HD], gate_rows], axis=0)

    def exchange(parts):
        return lax.all_to_all(parts, PLANE, split_axis=0, concat_axis=0, tiled=True)

    copies = jnp.broadcast_to(at_first[None], (COLUMNS,) + at_first.shape)
    plane_q = exchange(copies)
    plane_gates = plane_q[:, 2 * HC * HD : 2 * HC * HD + HEADS, 0:6].astype(jnp.int32)
    columns = jnp.arange(COLUMNS, dtype=jnp.int32)
    plane_gates = jnp.where((columns > column)[:, None, None], plane_gates, -1)
    plane_gates = jnp.where((columns == column)[:, None, None], gates, plane_gates)
    holders = jnp.arange(COLUMNS, dtype=jnp.int32) * RING + z
    head_range = jnp.arange(HEADS, dtype=jnp.int32)

    def table_of(places):
        blocks = column * RING + places
        named = jnp.any(plane_gates[:, :, None, 1:] == blocks[None, None, :, None], axis=-1)
        named = named & (blocks[None, None, :] != holders[:, None, None])
        table = jnp.sum(jnp.where(named, head_range[None, :, None] + 1, 0), axis=1) - 1
        return jnp.concatenate([table, jnp.full((1, RING), column, jnp.int32)], axis=0)

    ring_table = table_of((z + jnp.array([0, -1, 1, -2, 2, -3, 3, 4], jnp.int32) + RING) % RING)
    line_table = table_of(jnp.arange(RING, dtype=jnp.int32))

    own, own_lse = own_attention(queries, keys, values, copies)

    def weight_part(side, half):
        return lax.dynamic_slice_in_dim(out_weight, side * 2048 + half * 1024, 1024, axis=1)

    weights = [weight_part(s, c) for s in (1 - chip, chip) for c in (1 - core, core)]

    def gather_kv(part):
        return [lax.all_gather(part[None], "z", axis=0, tiled=True)]

    def start_kv(chunk, after):
        part = pack(chunk * HC, HC, [keys, values], after)
        return [part]

    def move_kv(ring, after=None):
        up, down = ring[-2:] if len(ring) > 1 else ring * 2
        if after is not None:
            up, down = hold(up, down, after)
        return ring + [shift(up, "z", RING, 1), shift(down, "z", RING, -1)]

    def complete_kv(ring, after):
        k_half, v_half = far_halves(ring[5], ring[6], after)
        return ring + [shift(k_half, "z", RING, 1), shift(v_half, "z", RING, -1)]

    first_column = column.reshape(1)

    def serve(chunk, table, q, q_row, following, kvs, after):
        return column_tasks(
            chunk, table - jnp.int32(chunk * HC) * below, q, q_row, q_turned, following, kvs, after
        )

    below = (jnp.arange(COLUMNS + 1) < COLUMNS).astype(jnp.int32)[:, None]
    def swap_core(array):
        return shift(array, "core", 2, 1)

    def swap_chip(array):
        return shift(array, "yl", 2, 1)

    def weight_part(first, last, side, half):
        return lax.dynamic_slice(out_weight, (first, (side * 2 + half) * 1024), (last - first, 1024))

    rows = HC * HD

    sides = (1 - chip, chip)
    weights = [(weight_part(0, HEADS * HD, side, core), swap_core(weight_part(0, HEADS * HD, side, 1 - core))) for side in sides]

    def project(chunk, count, features):
        both = jnp.concatenate([features, swap_core(features)], axis=0)
        place = slice(chunk * rows, (chunk + count) * rows)
        return [
            lax.dot_general(both, jnp.concatenate([w[place] for w in pair], axis=0), TN, preferred_element_type=jnp.float32)
            for pair in weights
        ]

    def merged(chunk, back):
        return merge(chunk, first_column, back, own, own_lse)

    ring0 = start_kv(0, [])
    ring2 = start_kv(2, ring0)
    ring3 = start_kv(3, ring2)
    kv0 = gather_kv(ring0[0])
    kv2 = gather_kv(ring2[0])
    kv3 = gather_kv(ring3[0])
    ring1 = move_kv(move_kv(start_kv(1, [own])))
    early = ring1[-2:]
    ring1 = move_kv(ring1)
    part0 = serve(0, line_table, plane_q, 0, 2, kv0, ring1[-2:])
    back0 = exchange(part0)
    kv1 = complete_kv(ring1, [part0])
    part1 = serve(1, ring_table, plane_q, HC * HD, 3, kv1, [part0])
    back1 = exchange(part1)
    part2 = serve(2, line_table, back0, 0, None, kv2, [part1])
    back2 = exchange(part2)
    sums = project(0, 2, jnp.concatenate([merged(0, back0), merged(1, back1)], axis=0))
    part3 = serve(3, line_table, back1, 0, None, kv3, [part2])
    back3 = exchange(part3)
    for chunk, back in ((2, back2), (3, back3)):
        sums = [a + b for a, b in zip(sums, project(chunk, 1, merged(chunk, back)))]
    away = swap_chip(sums[0].astype(jnp.bfloat16))
    return (sums[1] + away.astype(jnp.float32)).astype(jnp.bfloat16)


def solution(mesh):
    fine = Mesh(mesh.devices.reshape(2, 4, 8, 2, 2), SEQ + HEAD)
    placed = (
        P(SEQ, HEAD),
        P(SEQ, HEAD),
        P(SEQ, HEAD),
        P(SEQ, HEAD, None),
        P(HEAD, None),
    )
    return jax.shard_map(
        on_device, mesh=fine, in_specs=placed, out_specs=P(SEQ, HEAD), check_vma=False
    )
```

```python
import functools
import math

import jax
import jax.numpy as jnp
from jax import lax
from jax.experimental import pallas as pl
from jax.experimental.pallas import tpu as pltpu
from jax.sharding import Mesh
from jax.sharding import PartitionSpec as P

NEGATIVE = -1e30
HEADS = 8
HD = 128
ROWS = 512
COLUMNS = 8
RING = 8
STAT_ROWS = 16
HC = 2
CHUNKS = HEADS // HC
QB = 256
SCALE = HD**-0.5 * math.log2(math.e)
SEQ = ("yh", "x", "z")
HEAD = ("yl", "core")
PLANE = ("yh", "x")
NT = (((1,), (1,)), ((), ()))
TN = (((0,), (0,)), ((), ()))


def own_kernel(q_ref, k_ref, v_ref, _, o_ref, lse_ref):
    head = pl.program_id(0)
    k = k_ref[...]
    v = v_ref[...]
    for start in range(0, ROWS, QB):
        q = q_ref[start : start + QB, :]
        s = lax.dot_general(k, q, NT, preferred_element_type=jnp.float32)
        key_at = lax.broadcasted_iota(jnp.int32, s.shape, 0)
        query_at = lax.broadcasted_iota(jnp.int32, s.shape, 1) + start
        s = jnp.where(key_at <= query_at, s, NEGATIVE)
        top = jnp.max(s, axis=0, keepdims=True) * SCALE
        p = jnp.exp2(s * SCALE - top)
        total = jnp.sum(p, axis=0, keepdims=True)
        o = lax.dot_general(v, p.astype(jnp.bfloat16), TN, preferred_element_type=jnp.float32)
        o_ref[:, start : start + QB] = (o / total).astype(jnp.bfloat16)
        lse_ref[pl.ds(head, 1), start : start + QB] = top + jnp.log2(total)


def own_attention(q, k, v, after):
    block = pl.BlockSpec((ROWS, HD), lambda h: (0, h))
    return pl.pallas_call(
        own_kernel,
        grid=(HEADS,),
        in_specs=[block, block, block, pl.BlockSpec(memory_space=pltpu.HBM)],
        out_specs=[
            pl.BlockSpec((HD, ROWS), lambda h: (h, 0)),
            pl.BlockSpec((HEADS, ROWS), lambda h: (0, 0)),
        ],
        out_shape=[
            jax.ShapeDtypeStruct((HEADS * HD, ROWS), jnp.bfloat16),
            jax.ShapeDtypeStruct((HEADS, ROWS), jnp.float32),
        ],
        cost_estimate=pl.CostEstimate(
            flops=9 * 10**9, bytes_accessed=4 << 20, transcendentals=0
        ),
        name="own_block",
    )(q, k, v, after)


def task_kernel(q_row, kv_count, has_next, table, q_hbm, own_ref, *refs):
    heads = HC
    next_ref = refs[0] if has_next else None
    kv_hbm = refs[has_next : has_next + kv_count]
    o_ref, q_buf, kv_buf, acc, top, total, stat, scores, tops, tasks, sems = refs[-11:]
    own_column = table[COLUMNS, 0]
    moves = [(q_hbm.at[:, q_row : q_row + heads * HD], q_buf)]
    if kv_count == 1:
        moves += [(kv_hbm[0], kv_buf)]
    else:
        moves += [(kv_hbm[i], kv_buf.at[i]) for i in range(RING - 1)]
        moves += [(kv_hbm[RING - 1 + i], kv_buf.at[RING - 1, i]) for i in range(2)]
    copies = [pltpu.make_async_copy(*move, sems.at[i]) for i, move in enumerate(moves)]
    for copy in copies:
        copy.start()

    def clear(i, _):
        acc[i] = jnp.zeros((HD, ROWS), jnp.float32)
        return 0

    lax.fori_loop(0, COLUMNS * heads, clear, 0)
    top[...] = jnp.full_like(top, NEGATIVE)
    total[...] = jnp.zeros_like(total)

    def collect(i, count):
        head = table[i // RING, i % RING]
        wanted = (head >= 0) & (head < heads)

        @pl.when(wanted)
        def _():
            tasks[0, count] = i // RING
            tasks[1, count] = i % RING
            tasks[2, count] = head
            tasks[3, count] = (i // RING) * heads + head

        return count + wanted.astype(jnp.int32)

    count = lax.fori_loop(0, COLUMNS * RING, collect, 0)
    for extra in range(3):
        tasks[0, count + extra] = 0
        tasks[1, count + extra] = 0
        tasks[2, count + extra] = 0
        tasks[3, count + extra] = COLUMNS * heads
    for copy in copies:
        copy.wait()
    q_buf[own_column] = own_ref[...]

    def lanes(t):
        return pl.ds(pl.multiple_of(tasks[2, t] * HD, HD), HD)

    def score(t, slot):
        k = kv_buf[tasks[1, t], 0, :, lanes(t)]
        q = q_buf[tasks[0, t], lanes(t), :]
        s = jnp.dot(k, q, preferred_element_type=jnp.float32)
        scores[slot] = s
        tops[slot] = jnp.max(s, axis=0, keepdims=True) * SCALE

    def soften(t, slot):
        place = tasks[3, t]
        before = top[place]
        after = jnp.maximum(before, tops[slot])
        p = jnp.exp2(scores[slot] * SCALE - after)
        keep = jnp.exp2(before - after)
        top[place] = after
        total[place] = total[place] * keep + jnp.sum(p, axis=0, keepdims=True)
        v = kv_buf[tasks[1, t], 1, :, lanes(t)]
        o = lax.dot_general(v, p.astype(jnp.bfloat16), TN, preferred_element_type=jnp.float32)
        acc[place] = acc[place] * keep + o

    score(0, 0)

    def two(u, _):
        t = u * 2
        score(t + 1, 1)
        soften(t, 0)
        score(t + 2, 0)
        soften(t + 1, 1)
        return 0

    lax.fori_loop(0, (count + 1) // 2, two, 0)

    stat[...] = jnp.zeros_like(stat)

    def finish(column, _):
        for head in range(heads):
            place = column * heads + head
            sums = total[place]
            sums = jnp.where(sums > 0.0, sums, 1.0)
            o_ref[column, head * HD : (head + 1) * HD, :] = (acc[place] / sums).astype(jnp.bfloat16)
            lse = top[place] + jnp.log2(sums)
            first = lse.astype(jnp.bfloat16).astype(jnp.float32)
            second = (lse - first).astype(jnp.bfloat16).astype(jnp.float32)
            for piece, value in enumerate((first, second, lse - first - second)):
                row = piece * heads + head
                stat[row : row + 1, :] = value
        o_ref[column, heads * HD : heads * HD + STAT_ROWS, :] = stat[...].astype(jnp.bfloat16)
        return 0

    lax.fori_loop(own_column, COLUMNS, finish, 0)

    def forward(column, _):
        if has_next:
            o_ref[column, 0 : heads * HD, :] = next_ref[...]
        else:
            o_ref[column, 0 : heads * HD, :] = jnp.zeros((heads * HD, ROWS), jnp.bfloat16)
        o_ref[column, heads * HD : heads * HD + STAT_ROWS, :] = jnp.zeros((STAT_ROWS, ROWS), jnp.bfloat16)
        return 0

    lax.fori_loop(0, own_column, forward, 0)


def column_tasks(chunk, table, q, q_row, q_turned, following, kvs, after):
    heads = HC
    anywhere = pl.BlockSpec(memory_space=pltpu.HBM)
    turned = lambda at: pl.BlockSpec((heads * HD, ROWS), lambda i, t: (at, 0))
    rows = heads * HD + STAT_ROWS
    has_next = following is not None
    return pl.pallas_call(
        functools.partial(task_kernel, q_row, len(kvs), int(has_next)),
        grid_spec=pltpu.PrefetchScalarGridSpec(
            num_scalar_prefetch=1,
            grid=(1,),
            in_specs=[anywhere, turned(chunk)]
            + ([turned(following)] if has_next else [])
            + [anywhere] * (len(kvs) + len(after)),
            out_specs=pl.BlockSpec((COLUMNS, rows, ROWS), lambda i, t: (0, 0, 0)),
            scratch_shapes=[
                pltpu.VMEM((COLUMNS, heads * HD, ROWS), jnp.bfloat16),
                pltpu.VMEM((RING, 2, ROWS, heads * HD), jnp.bfloat16),
                pltpu.VMEM((COLUMNS * heads + 1, HD, ROWS), jnp.float32),
                pltpu.VMEM((COLUMNS * heads + 1, 1, ROWS), jnp.float32),
                pltpu.VMEM((COLUMNS * heads + 1, 1, ROWS), jnp.float32),
                pltpu.VMEM((STAT_ROWS, ROWS), jnp.float32),
                pltpu.VMEM((2, ROWS, ROWS), jnp.float32),
                pltpu.VMEM((2, 1, ROWS), jnp.float32),
                pltpu.SMEM((4, COLUMNS * RING + 8), jnp.int32),
                pltpu.SemaphoreType.DMA((RING + 2,)),
            ],
        ),
        out_shape=jax.ShapeDtypeStruct((COLUMNS, rows, ROWS), jnp.bfloat16),
        compiler_params=pltpu.CompilerParams(vmem_limit_bytes=56 << 20),
        cost_estimate=pl.CostEstimate(
            flops=heads * 4 * 10**9,
            bytes_accessed=heads * 4 << 20,
            transcendentals=0,
        ),
        name="column_tasks",
    )(table, q, q_turned, *([q_turned] if has_next else []), *kvs, *after)


def merge_kernel(first_head, column, part_ref, stat_ref, own_ref, own_lse_ref, o_ref):
    head = pl.program_id(0)
    row = lax.broadcasted_iota(jnp.int32, (STAT_ROWS, ROWS), 0)
    pick = (row < 3 * HC) & (row % HC == head)
    lse = []
    for i in range(COLUMNS):
        pieces = jnp.where(pick, stat_ref[i].astype(jnp.float32), 0.0)
        lse.append(jnp.where(i <= column[0], jnp.sum(pieces, axis=0, keepdims=True), NEGATIVE))
    own = own_lse_ref[pl.ds(first_head + head, 1), :]
    highest = own
    for l in lse:
        highest = jnp.maximum(highest, l)
    weight = jnp.exp2(own - highest)
    norm = weight
    out = weight * own_ref[...].astype(jnp.float32)
    for i in range(COLUMNS):
        weight = jnp.exp2(lse[i] - highest)
        norm = norm + weight
        out = out + weight * part_ref[i].astype(jnp.float32)
    o_ref[...] = (out / norm).astype(jnp.bfloat16)


def merge(chunk, column, parts, own, own_lse):
    return pl.pallas_call(
        functools.partial(merge_kernel, chunk * HC),
        grid_spec=pltpu.PrefetchScalarGridSpec(
            num_scalar_prefetch=1,
            grid=(HC,),
            in_specs=[
                pl.BlockSpec((COLUMNS, HD, ROWS), lambda h, c: (0, h, 0)),
                pl.BlockSpec((COLUMNS, STAT_ROWS, ROWS), lambda h, c: (0, HC * HD // STAT_ROWS, 0)),
                pl.BlockSpec((HD, ROWS), lambda h, c: (chunk * HC + h, 0)),
                pl.BlockSpec((HEADS, ROWS), lambda h, c: (0, 0)),
            ],
            out_specs=pl.BlockSpec((HD, ROWS), lambda h, c: (h, 0)),
        ),
        out_shape=jax.ShapeDtypeStruct((HC * HD, ROWS), jnp.bfloat16),
        compiler_params=pltpu.CompilerParams(vmem_limit_bytes=20 << 20),
        cost_estimate=pl.CostEstimate(flops=0, bytes_accessed=HC * 5 << 20, transcendentals=0),
        name="merge",
    )(column, parts, parts, own, own_lse)


def pack_kernel(*refs):
    o_ref = refs[-1]
    for i in range(o_ref.shape[0]):
        o_ref[i] = refs[i][...]


def pack(first, heads, arrays, after):
    block = pl.BlockSpec((ROWS, heads * HD), lambda i: (0, first // heads))
    shape = (len(arrays), ROWS, heads * HD)
    return pl.pallas_call(
        pack_kernel,
        grid=(1,),
        in_specs=[block] * len(arrays) + [pl.BlockSpec(memory_space=pltpu.HBM)] * len(after),
        out_specs=pl.BlockSpec(shape, lambda i: (0, 0, 0)),
        out_shape=jax.ShapeDtypeStruct(shape, jnp.bfloat16),
        cost_estimate=pl.CostEstimate(flops=0, bytes_accessed=heads << 20, transcendentals=0),
        name="pack",
    )(*arrays, *after)


def halves_kernel(up_ref, down_ref, *refs):
    k_ref, v_ref = refs[-2:]
    k_ref[...] = up_ref[0]
    v_ref[...] = down_ref[0]


def hold_kernel(up_ref, down_ref, *refs):
    for source, target in ((up_ref, refs[-2]), (down_ref, refs[-1])):
        target[...] = source[...]


def hold(up, down, after):
    whole = pl.BlockSpec(up.shape, lambda i: (0, 0, 0))
    return pl.pallas_call(
        hold_kernel,
        grid=(1,),
        in_specs=[whole, whole] + [pl.BlockSpec(memory_space=pltpu.HBM)] * len(after),
        out_specs=[whole, whole],
        out_shape=[jax.ShapeDtypeStruct(up.shape, up.dtype)] * 2,
        cost_estimate=pl.CostEstimate(flops=0, bytes_accessed=4 << 20, transcendentals=0),
        name="hold",
    )(up, down, *after)


def far_halves(up, down, after):
    shape = up.shape[1:]
    whole = pl.BlockSpec(shape, lambda i: (0, 0))
    return pl.pallas_call(
        halves_kernel,
        grid=(1,),
        in_specs=[
            pl.BlockSpec((1,) + shape, lambda i: (0, 0, 0)),
            pl.BlockSpec((1,) + shape, lambda i: (1, 0, 0)),
        ]
        + [pl.BlockSpec(memory_space=pltpu.HBM)] * len(after),
        out_specs=[whole, whole],
        out_shape=[jax.ShapeDtypeStruct(shape, up.dtype)] * 2,
        cost_estimate=pl.CostEstimate(flops=0, bytes_accessed=2 << 20, transcendentals=0),
        name="far_halves",
    )(up, down, *after)


def shift(array, axis, size, by):
    return lax.ppermute(array, axis, [(i, (i + by) % size) for i in range(size)])


def on_device(queries, keys, values, gates, out_weight):
    column = lax.axis_index("yh") * 4 + lax.axis_index("x")
    z = lax.axis_index("z")
    chip = lax.axis_index("yl")
    core = lax.axis_index("core")

    gate_rows = jnp.zeros((STAT_ROWS, ROWS), jnp.bfloat16)
    gate_rows = lax.dynamic_update_slice(gate_rows, gates[0].astype(jnp.bfloat16), (0, 0))
    q_turned = queries.T
    at_first = jnp.concatenate([q_turned[: 2 * HC * HD], gate_rows], axis=0)

    def exchange(parts):
        return lax.all_to_all(parts, PLANE, split_axis=0, concat_axis=0, tiled=True)

    copies = jnp.broadcast_to(at_first[None], (COLUMNS,) + at_first.shape)
    plane_q = exchange(copies)
    plane_gates = plane_q[:, 2 * HC * HD : 2 * HC * HD + HEADS, 0:6].astype(jnp.int32)
    columns = jnp.arange(COLUMNS, dtype=jnp.int32)
    plane_gates = jnp.where((columns > column)[:, None, None], plane_gates, -1)
    plane_gates = jnp.where((columns == column)[:, None, None], gates, plane_gates)
    holders = jnp.arange(COLUMNS, dtype=jnp.int32) * RING + z
    head_range = jnp.arange(HEADS, dtype=jnp.int32)

    def table_of(places):
        blocks = column * RING + places
        named = jnp.any(plane_gates[:, :, None, 1:] == blocks[None, None, :, None], axis=-1)
        named = named & (blocks[None, None, :] != holders[:, None, None])
        table = jnp.sum(jnp.where(named, head_range[None, :, None] + 1, 0), axis=1) - 1
        return jnp.concatenate([table, jnp.full((1, RING), column, jnp.int32)], axis=0)

    ring_table = table_of((z + jnp.array([0, -1, 1, -2, 2, -3, 3, 4], jnp.int32) + RING) % RING)
    line_table = table_of(jnp.arange(RING, dtype=jnp.int32))

    own, own_lse = own_attention(queries, keys, values, copies)

    def weight_part(side, half):
        return lax.dynamic_slice_in_dim(out_weight, side * 2048 + half * 1024, 1024, axis=1)

    weights = [weight_part(s, c) for s in (1 - chip, chip) for c in (1 - core, core)]

    def gather_kv(part):
        return [lax.all_gather(part[None], "z", axis=0, tiled=True)]

    def start_kv(chunk, after):
        part = pack(chunk * HC, HC, [keys, values], after)
        return [part]

    def move_kv(ring, after=None):
        up, down = ring[-2:] if len(ring) > 1 else ring * 2
        if after is not None:
            up, down = hold(up, down, after)
        return ring + [shift(up, "z", RING, 1), shift(down, "z", RING, -1)]

    def complete_kv(ring, after):
        k_half, v_half = far_halves(ring[5], ring[6], after)
        return ring + [shift(k_half, "z", RING, 1), shift(v_half, "z", RING, -1)]

    first_column = column.reshape(1)

    def serve(chunk, table, q, q_row, following, kvs, after):
        return column_tasks(
            chunk, table - jnp.int32(chunk * HC) * below, q, q_row, q_turned, following, kvs, after
        )

    below = (jnp.arange(COLUMNS + 1) < COLUMNS).astype(jnp.int32)[:, None]
    def swap_core(array):
        return shift(array, "core", 2, 1)

    def swap_chip(array):
        return shift(array, "yl", 2, 1)

    def weight_part(first, last, side, half):
        return lax.dynamic_slice(out_weight, (first, (side * 2 + half) * 1024), (last - first, 1024))

    rows = HC * HD

    sides = (1 - chip, chip)
    weights = [(weight_part(0, HEADS * HD, side, core), swap_core(weight_part(0, HEADS * HD, side, 1 - core))) for side in sides]

    def project(chunk, count, features):
        both = jnp.concatenate([features, swap_core(features)], axis=0)
        place = slice(chunk * rows, (chunk + count) * rows)
        return [
            lax.dot_general(both, jnp.concatenate([w[place] for w in pair], axis=0), TN, preferred_element_type=jnp.float32)
            for pair in weights
        ]

    def merged(chunk, back):
        return merge(chunk, first_column, back, own, own_lse)

    ring0 = start_kv(0, [])
    ring2 = start_kv(2, ring0)
    ring3 = start_kv(3, ring2)
    kv0 = gather_kv(ring0[0])
    kv2 = gather_kv(ring2[0])
    kv3 = gather_kv(ring3[0])
    ring1 = move_kv(move_kv(start_kv(1, [])))
    early = ring1[-2:]
    ring1 = move_kv(ring1)
    part0 = serve(0, line_table, plane_q, 0, 2, kv0, [own, *ring1[-2:]])
    back0 = exchange(part0)
    kv1 = complete_kv(ring1, [part0])
    part1 = serve(1, ring_table, plane_q, HC * HD, 3, kv1, [part0])
    back1 = exchange(part1)
    part2 = serve(2, line_table, back0, 0, None, kv2, [part1])
    back2 = exchange(part2)
    sums = project(0, 2, jnp.concatenate([merged(0, back0), merged(1, back1)], axis=0))
    part3 = serve(3, line_table, back1, 0, None, kv3, [part2])
    back3 = exchange(part3)
    for chunk, back in ((2, back2), (3, back3)):
        sums = [a + b for a, b in zip(sums, project(chunk, 1, merged(chunk, back)))]
    away = swap_chip(sums[0].astype(jnp.bfloat16))
    return (sums[1] + away.astype(jnp.float32)).astype(jnp.bfloat16)


def solution(mesh):
    fine = Mesh(mesh.devices.reshape(2, 4, 8, 2, 2), SEQ + HEAD)
    placed = (
        P(SEQ, HEAD),
        P(SEQ, HEAD),
        P(SEQ, HEAD),
        P(SEQ, HEAD, None),
        P(HEAD, None),
    )
    return jax.shard_map(
        on_device, mesh=fine, in_specs=placed, out_specs=P(SEQ, HEAD), check_vma=False
    )
```

```python
import functools
import math

import jax
import jax.numpy as jnp
from jax import lax
from jax.experimental import pallas as pl
from jax.experimental.pallas import tpu as pltpu
from jax.sharding import Mesh
from jax.sharding import PartitionSpec as P

NEGATIVE = -1e30
HEADS = 8
HD = 128
ROWS = 512
COLUMNS = 8
RING = 8
STAT_ROWS = 16
HC = 2
CHUNKS = HEADS // HC
QB = 256
SCALE = HD**-0.5 * math.log2(math.e)
SEQ = ("yh", "x", "z")
HEAD = ("yl", "core")
PLANE = ("yh", "x")
NT = (((1,), (1,)), ((), ()))
TN = (((0,), (0,)), ((), ()))


def own_kernel(q_ref, k_ref, v_ref, _, o_ref, lse_ref):
    head = pl.program_id(0)
    k = k_ref[...]
    v = v_ref[...]
    for start in range(0, ROWS, QB):
        q = q_ref[start : start + QB, :]
        s = lax.dot_general(k, q, NT, preferred_element_type=jnp.float32)
        key_at = lax.broadcasted_iota(jnp.int32, s.shape, 0)
        query_at = lax.broadcasted_iota(jnp.int32, s.shape, 1) + start
        s = jnp.where(key_at <= query_at, s, NEGATIVE)
        top = jnp.max(s, axis=0, keepdims=True) * SCALE
        p = jnp.exp2(s * SCALE - top)
        total = jnp.sum(p, axis=0, keepdims=True)
        o = lax.dot_general(v, p.astype(jnp.bfloat16), TN, preferred_element_type=jnp.float32)
        o_ref[:, start : start + QB] = (o / total).astype(jnp.bfloat16)
        lse_ref[pl.ds(head, 1), start : start + QB] = top + jnp.log2(total)


def own_attention(q, k, v, after):
    block = pl.BlockSpec((ROWS, HD), lambda h: (0, h))
    return pl.pallas_call(
        own_kernel,
        grid=(HEADS,),
        in_specs=[block, block, block, pl.BlockSpec(memory_space=pltpu.HBM)],
        out_specs=[
            pl.BlockSpec((HD, ROWS), lambda h: (h, 0)),
            pl.BlockSpec((HEADS, ROWS), lambda h: (0, 0)),
        ],
        out_shape=[
            jax.ShapeDtypeStruct((HEADS * HD, ROWS), jnp.bfloat16),
            jax.ShapeDtypeStruct((HEADS, ROWS), jnp.float32),
        ],
        cost_estimate=pl.CostEstimate(
            flops=9 * 10**9, bytes_accessed=4 << 20, transcendentals=0
        ),
        name="own_block",
    )(q, k, v, after)


def task_kernel(q_row, kv_count, has_next, table, q_hbm, own_ref, *refs):
    heads = HC
    next_ref = refs[0] if has_next else None
    kv_hbm = refs[has_next : has_next + kv_count]
    o_ref, q_buf, kv_buf, acc, top, total, stat, scores, tops, tasks, sems = refs[-11:]
    own_column = table[COLUMNS, 0]
    moves = [(q_hbm.at[:, q_row : q_row + heads * HD], q_buf)]
    if kv_count == 1:
        moves += [(kv_hbm[0], kv_buf)]
    else:
        moves += [(kv_hbm[i], kv_buf.at[i]) for i in range(RING - 1)]
        moves += [(kv_hbm[RING - 1 + i], kv_buf.at[RING - 1, i]) for i in range(2)]
    copies = [pltpu.make_async_copy(*move, sems.at[i]) for i, move in enumerate(moves)]
    for copy in copies:
        copy.start()

    def clear(i, _):
        acc[i] = jnp.zeros((HD, ROWS), jnp.float32)
        return 0

    lax.fori_loop(0, COLUMNS * heads, clear, 0)
    top[...] = jnp.full_like(top, NEGATIVE)
    total[...] = jnp.zeros_like(total)

    def collect(i, count):
        head = table[i // RING, i % RING]
        wanted = (head >= 0) & (head < heads)

        @pl.when(wanted)
        def _():
            tasks[0, count] = i // RING
            tasks[1, count] = i % RING
            tasks[2, count] = head
            tasks[3, count] = (i // RING) * heads + head

        return count + wanted.astype(jnp.int32)

    count = lax.fori_loop(0, COLUMNS * RING, collect, 0)
    for extra in range(3):
        tasks[0, count + extra] = 0
        tasks[1, count + extra] = 0
        tasks[2, count + extra] = 0
        tasks[3, count + extra] = COLUMNS * heads
    for copy in copies:
        copy.wait()
    q_buf[own_column] = own_ref[...]

    def lanes(t):
        return pl.ds(pl.multiple_of(tasks[2, t] * HD, HD), HD)

    def score(t, slot):
        k = kv_buf[tasks[1, t], 0, :, lanes(t)]
        q = q_buf[tasks[0, t], lanes(t), :]
        s = jnp.dot(k, q, preferred_element_type=jnp.float32)
        scores[slot] = s
        tops[slot] = jnp.max(s, axis=0, keepdims=True) * SCALE

    def soften(t, slot):
        place = tasks[3, t]
        before = top[place]
        after = jnp.maximum(before, tops[slot])
        p = jnp.exp2(scores[slot] * SCALE - after)
        keep = jnp.exp2(before - after)
        top[place] = after
        total[place] = total[place] * keep + jnp.sum(p, axis=0, keepdims=True)
        v = kv_buf[tasks[1, t], 1, :, lanes(t)]
        o = lax.dot_general(v, p.astype(jnp.bfloat16), TN, preferred_element_type=jnp.float32)
        acc[place] = acc[place] * keep + o

    score(0, 0)

    def two(u, _):
        t = u * 2
        score(t + 1, 1)
        soften(t, 0)
        score(t + 2, 0)
        soften(t + 1, 1)
        return 0

    lax.fori_loop(0, (count + 1) // 2, two, 0)

    stat[...] = jnp.zeros_like(stat)

    def finish(column, _):
        for head in range(heads):
            place = column * heads + head
            sums = total[place]
            sums = jnp.where(sums > 0.0, sums, 1.0)
            o_ref[column, head * HD : (head + 1) * HD, :] = (acc[place] / sums).astype(jnp.bfloat16)
            lse = top[place] + jnp.log2(sums)
            first = lse.astype(jnp.bfloat16).astype(jnp.float32)
            second = (lse - first).astype(jnp.bfloat16).astype(jnp.float32)
            for piece, value in enumerate((first, second, lse - first - second)):
                row = piece * heads + head
                stat[row : row + 1, :] = value
        o_ref[column, heads * HD : heads * HD + STAT_ROWS, :] = stat[...].astype(jnp.bfloat16)
        return 0

    lax.fori_loop(own_column, COLUMNS, finish, 0)

    def forward(column, _):
        if has_next:
            o_ref[column, 0 : heads * HD, :] = next_ref[...]
        else:
            o_ref[column, 0 : heads * HD, :] = jnp.zeros((heads * HD, ROWS), jnp.bfloat16)
        o_ref[column, heads * HD : heads * HD + STAT_ROWS, :] = jnp.zeros((STAT_ROWS, ROWS), jnp.bfloat16)
        return 0

    lax.fori_loop(0, own_column, forward, 0)


def column_tasks(chunk, table, q, q_row, q_turned, following, kvs, after):
    heads = HC
    anywhere = pl.BlockSpec(memory_space=pltpu.HBM)
    turned = lambda at: pl.BlockSpec((heads * HD, ROWS), lambda i, t: (at, 0))
    rows = heads * HD + STAT_ROWS
    has_next = following is not None
    return pl.pallas_call(
        functools.partial(task_kernel, q_row, len(kvs), int(has_next)),
        grid_spec=pltpu.PrefetchScalarGridSpec(
            num_scalar_prefetch=1,
            grid=(1,),
            in_specs=[anywhere, turned(chunk)]
            + ([turned(following)] if has_next else [])
            + [anywhere] * (len(kvs) + len(after)),
            out_specs=pl.BlockSpec((COLUMNS, rows, ROWS), lambda i, t: (0, 0, 0)),
            scratch_shapes=[
                pltpu.VMEM((COLUMNS, heads * HD, ROWS), jnp.bfloat16),
                pltpu.VMEM((RING, 2, ROWS, heads * HD), jnp.bfloat16),
                pltpu.VMEM((COLUMNS * heads + 1, HD, ROWS), jnp.float32),
                pltpu.VMEM((COLUMNS * heads + 1, 1, ROWS), jnp.float32),
                pltpu.VMEM((COLUMNS * heads + 1, 1, ROWS), jnp.float32),
                pltpu.VMEM((STAT_ROWS, ROWS), jnp.float32),
                pltpu.VMEM((2, ROWS, ROWS), jnp.float32),
                pltpu.VMEM((2, 1, ROWS), jnp.float32),
                pltpu.SMEM((4, COLUMNS * RING + 8), jnp.int32),
                pltpu.SemaphoreType.DMA((RING + 2,)),
            ],
        ),
        out_shape=jax.ShapeDtypeStruct((COLUMNS, rows, ROWS), jnp.bfloat16),
        compiler_params=pltpu.CompilerParams(vmem_limit_bytes=56 << 20),
        cost_estimate=pl.CostEstimate(
            flops=heads * 4 * 10**9,
            bytes_accessed=heads * 4 << 20,
            transcendentals=0,
        ),
        name="column_tasks",
    )(table, q, q_turned, *([q_turned] if has_next else []), *kvs, *after)


def merge_kernel(first_head, column, part_ref, stat_ref, own_ref, own_lse_ref, o_ref):
    head = pl.program_id(0)
    row = lax.broadcasted_iota(jnp.int32, (STAT_ROWS, ROWS), 0)
    pick = (row < 3 * HC) & (row % HC == head)
    lse = []
    for i in range(COLUMNS):
        pieces = jnp.where(pick, stat_ref[i].astype(jnp.float32), 0.0)
        lse.append(jnp.where(i <= column[0], jnp.sum(pieces, axis=0, keepdims=True), NEGATIVE))
    own = own_lse_ref[pl.ds(first_head + head, 1), :]
    highest = own
    for l in lse:
        highest = jnp.maximum(highest, l)
    weight = jnp.exp2(own - highest)
    norm = weight
    out = weight * own_ref[...].astype(jnp.float32)
    for i in range(COLUMNS):
        weight = jnp.exp2(lse[i] - highest)
        norm = norm + weight
        out = out + weight * part_ref[i].astype(jnp.float32)
    o_ref[...] = (out / norm).astype(jnp.bfloat16)


def merge(chunk, column, parts, own, own_lse):
    return pl.pallas_call(
        functools.partial(merge_kernel, chunk * HC),
        grid_spec=pltpu.PrefetchScalarGridSpec(
            num_scalar_prefetch=1,
            grid=(HC,),
            in_specs=[
                pl.BlockSpec((COLUMNS, HD, ROWS), lambda h, c: (0, h, 0)),
                pl.BlockSpec((COLUMNS, STAT_ROWS, ROWS), lambda h, c: (0, HC * HD // STAT_ROWS, 0)),
                pl.BlockSpec((HD, ROWS), lambda h, c: (chunk * HC + h, 0)),
                pl.BlockSpec((HEADS, ROWS), lambda h, c: (0, 0)),
            ],
            out_specs=pl.BlockSpec((HD, ROWS), lambda h, c: (h, 0)),
        ),
        out_shape=jax.ShapeDtypeStruct((HC * HD, ROWS), jnp.bfloat16),
        compiler_params=pltpu.CompilerParams(vmem_limit_bytes=20 << 20),
        cost_estimate=pl.CostEstimate(flops=0, bytes_accessed=HC * 5 << 20, transcendentals=0),
        name="merge",
    )(column, parts, parts, own, own_lse)


def pack_kernel(*refs):
    o_ref = refs[-1]
    for i in range(o_ref.shape[0]):
        o_ref[i] = refs[i][...]


def pack(first, heads, arrays, after):
    block = pl.BlockSpec((ROWS, heads * HD), lambda i: (0, first // heads))
    shape = (len(arrays), ROWS, heads * HD)
    return pl.pallas_call(
        pack_kernel,
        grid=(1,),
        in_specs=[block] * len(arrays) + [pl.BlockSpec(memory_space=pltpu.HBM)] * len(after),
        out_specs=pl.BlockSpec(shape, lambda i: (0, 0, 0)),
        out_shape=jax.ShapeDtypeStruct(shape, jnp.bfloat16),
        cost_estimate=pl.CostEstimate(flops=0, bytes_accessed=heads << 20, transcendentals=0),
        name="pack",
    )(*arrays, *after)


def halves_kernel(up_ref, down_ref, *refs):
    k_ref, v_ref = refs[-2:]
    k_ref[...] = up_ref[0]
    v_ref[...] = down_ref[0]


def hold_kernel(up_ref, down_ref, *refs):
    for source, target in ((up_ref, refs[-2]), (down_ref, refs[-1])):
        target[...] = source[...]


def hold(up, down, after):
    whole = pl.BlockSpec(up.shape, lambda i: (0, 0, 0))
    return pl.pallas_call(
        hold_kernel,
        grid=(1,),
        in_specs=[whole, whole] + [pl.BlockSpec(memory_space=pltpu.HBM)] * len(after),
        out_specs=[whole, whole],
        out_shape=[jax.ShapeDtypeStruct(up.shape, up.dtype)] * 2,
        cost_estimate=pl.CostEstimate(flops=0, bytes_accessed=4 << 20, transcendentals=0),
        name="hold",
    )(up, down, *after)


def far_halves(up, down, after):
    shape = up.shape[1:]
    whole = pl.BlockSpec(shape, lambda i: (0, 0))
    return pl.pallas_call(
        halves_kernel,
        grid=(1,),
        in_specs=[
            pl.BlockSpec((1,) + shape, lambda i: (0, 0, 0)),
            pl.BlockSpec((1,) + shape, lambda i: (1, 0, 0)),
        ]
        + [pl.BlockSpec(memory_space=pltpu.HBM)] * len(after),
        out_specs=[whole, whole],
        out_shape=[jax.ShapeDtypeStruct(shape, up.dtype)] * 2,
        cost_estimate=pl.CostEstimate(flops=0, bytes_accessed=2 << 20, transcendentals=0),
        name="far_halves",
    )(up, down, *after)


def shift(array, axis, size, by):
    return lax.ppermute(array, axis, [(i, (i + by) % size) for i in range(size)])


def on_device(queries, keys, values, gates, out_weight):
    column = lax.axis_index("yh") * 4 + lax.axis_index("x")
    z = lax.axis_index("z")
    chip = lax.axis_index("yl")
    core = lax.axis_index("core")

    gate_rows = jnp.zeros((STAT_ROWS, ROWS), jnp.bfloat16)
    gate_rows = lax.dynamic_update_slice(gate_rows, gates[0].astype(jnp.bfloat16), (0, 0))
    q_turned = queries.T
    at_first = jnp.concatenate([q_turned[: 2 * HC * HD], gate_rows], axis=0)

    def exchange(parts):
        return lax.all_to_all(parts, PLANE, split_axis=0, concat_axis=0, tiled=True)

    copies = jnp.broadcast_to(at_first[None], (COLUMNS,) + at_first.shape)
    plane_q = exchange(copies)
    plane_gates = plane_q[:, 2 * HC * HD : 2 * HC * HD + HEADS, 0:6].astype(jnp.int32)
    columns = jnp.arange(COLUMNS, dtype=jnp.int32)
    plane_gates = jnp.where((columns > column)[:, None, None], plane_gates, -1)
    plane_gates = jnp.where((columns == column)[:, None, None], gates, plane_gates)
    holders = jnp.arange(COLUMNS, dtype=jnp.int32) * RING + z
    head_range = jnp.arange(HEADS, dtype=jnp.int32)

    def table_of(places):
        blocks = column * RING + places
        named = jnp.any(plane_gates[:, :, None, 1:] == blocks[None, None, :, None], axis=-1)
        named = named & (blocks[None, None, :] != holders[:, None, None])
        table = jnp.sum(jnp.where(named, head_range[None, :, None] + 1, 0), axis=1) - 1
        return jnp.concatenate([table, jnp.full((1, RING), column, jnp.int32)], axis=0)

    ring_table = table_of((z + jnp.array([0, -1, 1, -2, 2, -3, 3, 4], jnp.int32) + RING) % RING)
    line_table = table_of(jnp.arange(RING, dtype=jnp.int32))

    own, own_lse = own_attention(queries, keys, values, copies)

    def weight_part(side, half):
        return lax.dynamic_slice_in_dim(out_weight, side * 2048 + half * 1024, 1024, axis=1)

    weights = [weight_part(s, c) for s in (1 - chip, chip) for c in (1 - core, core)]

    def gather_kv(part):
        return [lax.all_gather(part[None], "z", axis=0, tiled=True)]

    def start_kv(chunk, after):
        part = pack(chunk * HC, HC, [keys, values], after)
        return [part]

    def move_kv(ring, after=None):
        up, down = ring[-2:] if len(ring) > 1 else ring * 2
        if after is not None:
            up, down = hold(up, down, after)
        return ring + [shift(up, "z", RING, 1), shift(down, "z", RING, -1)]

    def complete_kv(ring, after):
        k_half, v_half = far_halves(ring[5], ring[6], after)
        return ring + [shift(k_half, "z", RING, 1), shift(v_half, "z", RING, -1)]

    first_column = column.reshape(1)

    def serve(chunk, table, q, q_row, following, kvs, after):
        return column_tasks(
            chunk, table - jnp.int32(chunk * HC) * below, q, q_row, q_turned, following, kvs, after
        )

    below = (jnp.arange(COLUMNS + 1) < COLUMNS).astype(jnp.int32)[:, None]
    def swap_core(array):
        return shift(array, "core", 2, 1)

    def swap_chip(array):
        return shift(array, "yl", 2, 1)

    def weight_part(first, last, side, half):
        return lax.dynamic_slice(out_weight, (first, (side * 2 + half) * 1024), (last - first, 1024))

    rows = HC * HD

    sides = (1 - chip, chip)
    weights = [(weight_part(0, HEADS * HD, side, core), swap_core(weight_part(0, HEADS * HD, side, 1 - core))) for side in sides]

    def project(chunk, count, features):
        both = jnp.concatenate([features, swap_core(features)], axis=0)
        place = slice(chunk * rows, (chunk + count) * rows)
        return [
            lax.dot_general(both, jnp.concatenate([w[place] for w in pair], axis=0), TN, preferred_element_type=jnp.float32)
            for pair in weights
        ]

    def merged(chunk, back):
        return merge(chunk, first_column, back, own, own_lse)

    ring0 = start_kv(0, [])
    ring2 = start_kv(2, ring0)
    ring3 = start_kv(3, ring2)
    kv0 = gather_kv(ring0[0])
    kv2 = gather_kv(ring2[0])
    kv3 = gather_kv(ring3[0])
    ring1 = move_kv(move_kv(start_kv(1, [own, weights[0][1], weights[1][1]])))
    early = ring1[-2:]
    ring1 = move_kv(ring1)
    part0 = serve(0, line_table, plane_q, 0, 2, kv0, ring1[-2:])
    back0 = exchange(part0)
    kv1 = complete_kv(ring1, [part0])
    part1 = serve(1, ring_table, plane_q, HC * HD, 3, kv1, [part0])
    back1 = exchange(part1)
    part2 = serve(2, line_table, back0, 0, None, kv2, [part1])
    back2 = exchange(part2)
    sums = project(0, 2, jnp.concatenate([merged(0, back0), merged(1, back1)], axis=0))
    part3 = serve(3, line_table, back1, 0, None, kv3, [part2])
    back3 = exchange(part3)
    for chunk, back in ((2, back2), (3, back3)):
        sums = [a + b for a, b in zip(sums, project(chunk, 1, merged(chunk, back)))]
    away = swap_chip(sums[0].astype(jnp.bfloat16))
    return (sums[1] + away.astype(jnp.float32)).astype(jnp.bfloat16)


def solution(mesh):
    fine = Mesh(mesh.devices.reshape(2, 4, 8, 2, 2), SEQ + HEAD)
    placed = (
        P(SEQ, HEAD),
        P(SEQ, HEAD),
        P(SEQ, HEAD),
        P(SEQ, HEAD, None),
        P(HEAD, None),
    )
    return jax.shard_map(
        on_device, mesh=fine, in_specs=placed, out_specs=P(SEQ, HEAD), check_vma=False
    )
```
